128 devices in a mesh: fsdp: 16 (over x_lo, y, core), tp: 8 (over x_hi, z).
Axes of the slice: x: 4 (x_hi: 2, x_lo: 2; x = x_hi * 2 + x_lo), y: 4, z: 4, core: 2. Of those that a mesh axis runs over, the one named last changes fastest.
Arguments:
- master: float32 [8192, 10240], P(('fsdp', 'tp')), may hold values from -0.0625 to 0.0625
- moment: float32 [8192, 10240], P(('fsdp', 'tp')), may hold values from -0.02 to 0.02
- second: float32 [8192, 10240], P(('fsdp', 'tp')), may hold values from 1e-06 to 0.0001
- grad: bfloat16 [8192, 10240], P(('fsdp', 'tp')), may hold values from -0.019897461 to 0.019897461
- hidden: bfloat16 [64, 4, 8192], P('fsdp'), may hold values from -6 to 6
- cache: bfloat16 [64, 8, 2, 4096, 128], P('fsdp', 'tp'), may hold values from -400 to 400
- lengths: int32 [64], P('fsdp'), may hold values from 1 to 4096, as said below
- recorded: float32 [64, 4], P('fsdp'), may hold values from 5 to 10
- versions: int32 [64], P('fsdp'), may hold values from 0 to 3, as said below
Outputs:
- new_master: float32 [8192, 10240], P(('fsdp', 'tp'))
- attention: bfloat16 [64, 4, 8192], P('fsdp', None, 'tp')
- ratios: float32 [64, 4], P('fsdp')
- version_means: float32 [4], replicated
The draws below stay inside these ranges and needn't reach their ends.
Inputs may be any that keep to these rules, and one draw needn't show every extreme that they name: `lengths`: every row has at least one live slot; some row fills all 4096 slots. `versions`: some version may be named by no row.
All inputs are finite; a program needn't handle non-finite values.
Results may differ from the reference program's by a relative error of at most 0.0059.
The reference program's roundings to bfloat16 on the way count: a program that leaves them out, or rounds other values in their place, can miss the bound.
Values may be sent and summed in bfloat16 or wider, within the bound.
No kernel may reach another device: no remote copies, remote signals or barrier semaphores. Data moves between devices by JAX's collectives and lax.ppermute only.
A program may use at most 128 MiB of HBM per device.

```python
import math
import jax
import jax.numpy as jnp
from jax import lax

D = 8192
H = 64
KVH = 8
HD = 128
CACHE = 4096
STEPS = 4
VERSIONS = 4
ROWS = 64
E = 10240
N_TP = 8


def draw_cache(key, part):
    key = jax.random.fold_in(key, 11)
    base = jax.random.normal(key, (ROWS, KVH, 2, CACHE, HD), jnp.float32)
    return jnp.clip(base, -400.0, 400.0).astype(jnp.bfloat16)


def draw_lengths(key, part):
    key = jax.random.fold_in(key, 12)
    drawn = jax.random.randint(key, (ROWS,), 1, CACHE + 1)
    fullrow = jax.random.randint(jax.random.fold_in(key, 1), (), 0, ROWS)
    return drawn.at[fullrow].set(CACHE).astype(jnp.int32)


def draw_versions(key, part):
    key = jax.random.fold_in(key, 13)
    absent = jax.random.randint(jax.random.fold_in(key, 1), (), 1, VERSIONS - 1)
    drawn = jax.random.randint(key, (ROWS,), 0, VERSIONS - 1)
    shifted = jnp.where(drawn >= absent, drawn + 1, drawn)
    return shifted.astype(jnp.int32)


def level_of(key, shape, shards, smallest, high):
    loudness = 1.0
    for axis_at, blocks in shards:
        draws = jax.random.uniform(jax.random.fold_in(jax.random.fold_in(key, 6), axis_at), (blocks,), jnp.float32, smallest / len(shards), high / len(shards))
        loudness = loudness * jnp.repeat(jnp.exp(draws), shape[axis_at] // blocks).reshape((-1,) + (1,) * (len(shape) - 1 - axis_at))
    return loudness


def normal_values(stream_key, dims, width, limit, cuts=(), kind=jnp.bfloat16):
    factor_of = level_of(stream_key, dims, cuts, -0.22, 0.18) if cuts else 1.0
    values = jax.random.normal(stream_key, dims, jnp.float32) * width * factor_of
    return jnp.minimum(jnp.maximum(values, -limit), limit).astype(kind)


def setup_inputs(seed: int = 0) -> dict:
    key_list = jax.random.split(jax.random.key(seed), 10)
    return {
        "master": normal_values(key_list[0], (D, E), D ** -0.5, 0.0625, ((0, 128),), jnp.float32),
        "moment": normal_values(key_list[1], (D, E), 0.003, 0.02, ((0, 128),), jnp.float32),
        "second": jnp.clip(jnp.exp(math.log(0.0001) - 4.6051702 * jax.random.uniform(key_list[2], (D, E), jnp.float32) ** level_of(key_list[2], (D, E), ((0, 128),), -0.2, 0.2)), 9.999999974752427e-07, 0.0001),
        "grad": normal_values(key_list[3], (D, E), 0.003, 0.019897461, ((0, 128),)),
        "hidden": normal_values(key_list[4], (ROWS, STEPS, D), 1.0, 6.0, ((0, 16),)),
        "cache": draw_cache(jax.random.fold_in(key_list[9], 71), 0),
        "lengths": draw_lengths(jax.random.fold_in(key_list[9], 71), 0),
        "recorded": jnp.clip(5.0 + 5.0 * jax.random.uniform(key_list[7], (ROWS, STEPS), jnp.float32) ** level_of(key_list[7], (ROWS, STEPS), ((0, 16),), -0.2, 0.2), 5.0, 10.0),
        "versions": draw_versions(jax.random.fold_in(key_list[9], 71), 0),
    }


def adam_update(master, moment, second, grad):
    gradient = grad.astype(jnp.float32)
    fresh_moment = 0.9 * moment + 0.1 * gradient
    fresh_second = 0.95 * second + 0.05 * gradient * gradient
    corrected = fresh_moment / (1.0 - 0.9 ** 10)
    spread = jnp.sqrt(fresh_second / (1.0 - 0.95 ** 10)) + 1e-08
    return master - 0.005 * corrected / spread

def reference(master, moment, second, grad, hidden, cache, lengths, recorded, versions):
    new_master = adam_update(master, moment, second, grad)
    weights = new_master.astype(jnp.bfloat16)
    local_heads = H // N_TP
    local_kv = KVH // N_TP
    group = H // KVH
    qkv = jnp.dot(hidden.reshape(ROWS * STEPS, D), weights, preferred_element_type=jnp.float32)
    qkv = qkv.reshape(ROWS, STEPS, N_TP, local_heads + 2 * local_kv, HD)
    scale = HD ** (-0.5)

    def one_row(item):
        qkv_row, cache_row, length = item
        queries = qkv_row[:, :, :local_heads].astype(jnp.bfloat16).reshape(STEPS, KVH, group, HD).astype(jnp.float32)
        new_keys = qkv_row[:, :, local_heads:local_heads + local_kv].astype(jnp.bfloat16).reshape(STEPS, KVH, HD).astype(jnp.float32)
        new_values = qkv_row[:, :, local_heads + local_kv:].astype(jnp.bfloat16).reshape(STEPS, KVH, HD).astype(jnp.float32)
        old_keys = cache_row[:, 0].astype(jnp.float32)
        old_values = cache_row[:, 1].astype(jnp.float32)
        cache_scores = jnp.einsum('sgqd,gcd->sgqc', queries, old_keys) * scale
        slot_live = jnp.arange(CACHE, dtype=jnp.int32) < length
        cache_scores = jnp.where(slot_live[None, None, None, :], cache_scores, -1e+30)
        new_scores = jnp.einsum('sgqd,tgd->sgqt', queries, new_keys) * scale
        causal = jnp.arange(STEPS)[:, None] >= jnp.arange(STEPS)[None, :]
        new_scores = jnp.where(causal[:, None, None, :], new_scores, -1e+30)
        top = jnp.maximum(lax.optimization_barrier(jnp.max(cache_scores, axis=-1)), lax.optimization_barrier(jnp.max(new_scores, axis=-1)))
        cache_exp = jnp.exp(cache_scores - top[..., None])
        new_exp = jnp.exp(new_scores - top[..., None])
        total = lax.optimization_barrier(jnp.sum(cache_exp, axis=-1)) + lax.optimization_barrier(jnp.sum(new_exp, axis=-1))
        lse = top + jnp.log(total)
        cache_probs = (cache_exp / total[..., None]).astype(jnp.bfloat16).astype(jnp.float32)
        new_probs = (new_exp / total[..., None]).astype(jnp.bfloat16).astype(jnp.float32)
        output = jnp.einsum('sgqc,gcd->sgqd', cache_probs, old_values) + jnp.einsum('sgqt,tgd->sgqd', new_probs, new_values)
        return (output.reshape(STEPS, H * HD).astype(jnp.bfloat16), lax.optimization_barrier(jnp.sum(lse.reshape(STEPS, H), axis=-1)))
    attention, lse_sums = lax.map(one_row, (qkv, cache, lengths))
    normalizer = lse_sums / H
    ratios = jnp.exp(jnp.clip(normalizer - recorded, -2.0, 2.0))
    onehot = (versions[:, None] == jnp.arange(VERSIONS, dtype=jnp.int32)[None, :]).astype(jnp.float32)
    sums = lax.optimization_barrier(jnp.sum(lax.optimization_barrier(jnp.sum(ratios, axis=1))[:, None] * onehot, axis=0))
    counts = lax.optimization_barrier(jnp.sum(onehot, axis=0)) * STEPS
    version_means = sums / jnp.maximum(counts, 1.0)
    return (new_master, attention, ratios, version_means)
```

```python
import functools

import jax
import jax.numpy as jnp
from jax import lax
from jax.experimental import pallas as pl
from jax.experimental.pallas import tpu as pltpu
from jax.sharding import PartitionSpec as P

H = 64
HD = 128
VERSIONS = 4
F32 = jnp.float32
BF16 = jnp.bfloat16


def adam_kernel(master_ref, moment_ref, second_ref, grad_ref, new_ref, weight_ref):
    gradient = grad_ref[...].astype(F32)
    fresh_moment = 0.9 * moment_ref[...] + 0.1 * gradient
    fresh_second = 0.95 * second_ref[...] + 0.05 * gradient * gradient
    spread = jnp.sqrt(fresh_second / (1.0 - 0.95**10)) + 1e-08
    fresh = master_ref[...] - (0.005 / (1.0 - 0.9**10)) * fresh_moment / spread
    new_ref[...] = fresh
    weight_ref[0] = fresh.astype(BF16)


def adam(master, moment, second, grad, n_tp):
    rows, columns = master.shape
    width = columns // n_tp
    block = pl.BlockSpec((rows, width), lambda i: (0, i))
    return pl.pallas_call(
        adam_kernel,
        grid=(n_tp,),
        in_specs=[block] * 4,
        out_specs=[block, pl.BlockSpec((1, rows, width), lambda i: (i, 0, 0))],
        out_shape=[
            jax.ShapeDtypeStruct((rows, columns), F32),
            jax.ShapeDtypeStruct((n_tp, rows, width), BF16),
        ],
        compiler_params=pltpu.CompilerParams(vmem_limit_bytes=24 << 20),
        cost_estimate=pl.CostEstimate(
            flops=12 * rows * columns, bytes_accessed=20 * rows * columns, transcendentals=0
        ),
        name="adam",
    )(master, moment, second, grad)


def attention_kernel(heads, steps, copies, lengths_ref, parts_ref, cache_ref, out_ref, lse_ref, qkv):
    row = pl.program_id(0)

    @pl.when(row == 0)
    def _():
        total = parts_ref[0]
        for i in range(1, parts_ref.shape[0]):
            total = total + parts_ref[i]
        qkv[...] = total.reshape(qkv.shape)
        lse_ref[...] = jnp.zeros_like(lse_ref)

    mine = qkv[row]
    queries = jnp.concatenate(
        [mine[:, h * HD : (h + 1) * HD] for h in range(heads)], axis=0
    ).astype(BF16)
    new_keys = mine[:, heads * HD : (heads + 1) * HD].astype(BF16)
    new_values = mine[:, (heads + 1) * HD :].astype(BF16)
    scale = HD ** (-0.5)
    contract = (((1,), (1,)), ((), ()))
    scores = lax.dot_general(queries, cache_ref[0, 0, 0], contract, preferred_element_type=F32) * scale
    slot = lax.broadcasted_iota(jnp.int32, scores.shape, 1)
    scores = jnp.where(slot < lengths_ref[row], scores, -1e30)
    fresh = lax.dot_general(queries, new_keys, contract, preferred_element_type=F32) * scale
    step = lax.broadcasted_iota(jnp.int32, fresh.shape, 0) % steps
    later = lax.broadcasted_iota(jnp.int32, fresh.shape, 1)
    fresh = jnp.where(later <= step, fresh, -1e30)
    top = jnp.maximum(
        jnp.max(scores, axis=1, keepdims=True), jnp.max(fresh, axis=1, keepdims=True)
    )
    scores = jnp.exp(scores - top)
    fresh = jnp.exp(fresh - top)
    total = jnp.sum(scores, axis=1, keepdims=True) + jnp.sum(fresh, axis=1, keepdims=True)
    lse = top + jnp.log(total)
    inverse = 1.0 / total
    output = jnp.dot(
        (scores * inverse).astype(BF16), cache_ref[0, 0, 1], preferred_element_type=F32
    ) + jnp.dot((fresh * inverse).astype(BF16), new_values, preferred_element_type=F32)
    output = output.astype(BF16)
    out_ref[0] = jnp.concatenate(
        [output[h * steps : (h + 1) * steps] for h in range(heads)], axis=1
    )
    place = lax.broadcasted_iota(jnp.int32, (heads * steps, 128), 0) % steps
    lane = lax.broadcasted_iota(jnp.int32, (heads * steps, 128), 1)
    line = jnp.sum(jnp.where(place == lane, lse, 0.0), axis=0, keepdims=True)
    for c in range(copies):
        lse_ref[c, pl.ds(row, 1), :] = line


def attend(parts, cache, lengths, copies):
    rows, _, _, slots, _ = cache.shape
    count, tall, width = parts.shape
    steps = tall // rows
    heads = width // HD - 2
    return pl.pallas_call(
        functools.partial(attention_kernel, heads, steps, copies),
        grid_spec=pltpu.PrefetchScalarGridSpec(
            num_scalar_prefetch=1,
            grid=(rows,),
            in_specs=[
                pl.BlockSpec((count, tall, width), lambda r, s: (0, 0, 0)),
                pl.BlockSpec((1, 1, 2, slots, HD), lambda r, s: (r, 0, 0, 0, 0)),
            ],
            out_specs=[
                pl.BlockSpec((1, steps, heads * HD), lambda r, s: (r, 0, 0)),
                pl.BlockSpec((copies, 8, 128), lambda r, s: (0, 0, 0)),
            ],
            scratch_shapes=[pltpu.VMEM((rows, steps, width), F32)],
        ),
        out_shape=[
            jax.ShapeDtypeStruct((rows, steps, heads * HD), BF16),
            jax.ShapeDtypeStruct((copies, 8, 128), F32),
        ],
        compiler_params=pltpu.CompilerParams(vmem_limit_bytes=24 << 20),
        cost_estimate=pl.CostEstimate(
            flops=4 * rows * heads * steps * slots * HD,
            bytes_accessed=cache.size * 2,
            transcendentals=rows * heads * steps * slots,
        ),
        name="attend",
    )(lengths, parts, cache)


def ratio_kernel(copies, versions_ref, sums_ref, recorded_ref, ratios_ref, out_ref):
    rows, steps = recorded_ref.shape
    normalizer = jnp.sum(sums_ref[...], axis=0)[:rows, :steps] / H
    ratios = jnp.exp(jnp.clip(normalizer - recorded_ref[...], -2.0, 2.0))
    ratios_ref[...] = ratios
    per_row = jnp.sum(ratios, axis=1, keepdims=True)
    lane = lax.broadcasted_iota(jnp.int32, (1, 128), 1)
    sums = jnp.zeros((1, 128), F32)
    counts = jnp.zeros((1, 128), F32)
    for r in range(rows):
        hit = lane == versions_ref[r]
        sums = sums + jnp.where(hit, per_row[r : r + 1], 0.0)
        counts = counts + jnp.where(hit, float(steps), 0.0)
    line = lax.broadcasted_iota(jnp.int32, (8, 128), 0)
    both = jnp.where(line == 0, sums, jnp.where(line == 1, counts, 0.0))
    for c in range(copies):
        out_ref[c] = both


def ratio_sums(sums, recorded, versions, copies):
    return pl.pallas_call(
        functools.partial(ratio_kernel, copies),
        in_specs=[
            pl.BlockSpec(memory_space=pltpu.SMEM),
            pl.BlockSpec(memory_space=pltpu.VMEM),
            pl.BlockSpec(memory_space=pltpu.VMEM),
        ],
        out_specs=[pl.BlockSpec(memory_space=pltpu.VMEM)] * 2,
        out_shape=[
            jax.ShapeDtypeStruct(recorded.shape, F32),
            jax.ShapeDtypeStruct((copies, 8, 128), F32),
        ],
        name="ratio_sums",
    )(versions, sums, recorded)


def shards(master, moment, second, grad, hidden, cache, lengths, recorded, versions):
    n_tp = lax.axis_size("tp")
    n_fsdp = lax.axis_size("fsdp")
    rows, steps, width = hidden.shape
    tall = rows * steps
    depth = width // n_fsdp
    core = lax.axis_index("fsdp") % 2
    cores = [[i for i in range(n_fsdp) if i % 2 == c] for c in range(2)]
    pairs = [(i, i ^ 1) for i in range(n_fsdp)]
    chips = n_fsdp // 2

    spread = hidden.reshape(tall, n_fsdp, depth).transpose(1, 0, 2)
    spread = lax.all_to_all(spread, "fsdp", 0, 0, tiled=True).reshape(chips, 2, tall, depth)
    to_keep = lax.dynamic_index_in_dim(spread, core, 1, keepdims=False).reshape(-1, depth)
    to_send = lax.dynamic_index_in_dim(spread, 1 - core, 1, keepdims=False).reshape(-1, depth)

    new_master, fresh = adam(master, moment, second, grad, n_tp)
    weights = lax.all_to_all(fresh, "tp", 0, 0, tiled=True).reshape(depth, -1)
    sent = jnp.dot(to_send, weights, preferred_element_type=F32)
    arrived = lax.ppermute(sent, "fsdp", pairs)
    partial = jnp.dot(to_keep, weights, preferred_element_type=F32) + arrived
    parts = lax.all_to_all(
        partial.reshape(chips, tall, -1), "fsdp", 0, 0, tiled=True, axis_index_groups=cores
    )
    attention, lse_sums = attend(parts, cache, lengths, n_tp)
    lse_sums = lax.all_to_all(lse_sums, "tp", 0, 0, tiled=True)
    ratios, version_sums = ratio_sums(lse_sums, recorded, versions, n_fsdp)
    version_sums = jnp.sum(lax.all_to_all(version_sums, "fsdp", 0, 0, tiled=True), axis=0)
    version_means = version_sums[0, :VERSIONS] / jnp.maximum(version_sums[1, :VERSIONS], 1.0)
    return (new_master, attention, ratios, version_means)


def solution(mesh):
    in_specs = (
        P(("fsdp", "tp"), None),
        P(("fsdp", "tp"), None),
        P(("fsdp", "tp"), None),
        P(("fsdp", "tp"), None),
        P("fsdp", None, None),
        P("fsdp", "tp", None, None, None),
        P("fsdp"),
        P("fsdp", None),
        P("fsdp"),
    )
    out_specs = (P(("fsdp", "tp"), None), P("fsdp", None, "tp"), P("fsdp", None), P())
    return jax.shard_map(shards, mesh=mesh, in_specs=in_specs, out_specs=out_specs, check_vma=False)
```

```python
import functools

import jax
import jax.numpy as jnp
from jax import lax
from jax.experimental import pallas as pl
from jax.experimental.pallas import tpu as pltpu
from jax.sharding import PartitionSpec as P

H = 64
HD = 128
VERSIONS = 4
F32 = jnp.float32
BF16 = jnp.bfloat16
ANY = pl.BlockSpec(memory_space=pl.ANY)
VMEM = pl.BlockSpec(memory_space=pltpu.VMEM)
SMEM = pl.BlockSpec(memory_space=pltpu.SMEM)
MIB = 1 << 20
in_hbm = functools.partial(pltpu.with_memory_space_constraint, memory_space=pltpu.HBM)
in_vmem = functools.partial(pltpu.with_memory_space_constraint, memory_space=pltpu.VMEM)
LOG2E = 1.4426950408889634
AHEAD = 3
HOPS = (8, 1, 2, 6)


def adam_kernel(master, moment, second, grad, new, weights, a, b, c, g, n, w, arrive, leave):
    parts, rows, width = w.shape
    sources = ((master, a), (moment, b), (second, c), (grad, g))

    def columns(i):
        return pl.ds(i * width, width)

    def fetches(i):
        return [
            pltpu.make_async_copy(hbm.at[:, columns(i)], buf.at[i], arrive.at[i, k])
            for k, (hbm, buf) in enumerate(sources)
        ]

    def stores(i):
        return [
            pltpu.make_async_copy(n.at[i], new.at[:, columns(i)], leave.at[i, 0]),
            pltpu.make_async_copy(w.at[i], weights.at[i], leave.at[i, 1]),
        ]

    for i in range(AHEAD):
        for copy in fetches(i):
            copy.start()
    for i in range(parts):
        if i + AHEAD < parts:
            for copy in fetches(i + AHEAD):
                copy.start()
        for copy in fetches(i):
            copy.wait()

        def tile(k, carry, i=i):
            at = pl.ds(pl.multiple_of(k * 16, 16), 16)
            gradient = g[i, at].astype(F32)
            fresh_moment = 0.9 * b[i, at] + 0.1 * gradient
            fresh_second = 0.95 * c[i, at] + 0.05 * gradient * gradient
            spread = jnp.sqrt(fresh_second * (1.0 / (1.0 - 0.95**10))) + 1e-08
            fresh = a[i, at] - (0.005 / (1.0 - 0.9**10)) * fresh_moment / spread
            n[i, at] = fresh
            w[i, at] = fresh.astype(BF16)
            return carry

        lax.fori_loop(0, rows // 16, tile, 0)
        for copy in stores(i):
            copy.start()
    for i in range(parts):
        for copy in stores(i):
            copy.wait()


def adam(master, moment, second, grad, parts):
    rows, columns = master.shape
    width = columns // parts
    return pl.pallas_call(
        adam_kernel,
        in_specs=[ANY] * 4,
        out_specs=[ANY] * 2,
        out_shape=[
            jax.ShapeDtypeStruct((rows, columns), F32),
            jax.ShapeDtypeStruct((parts, rows, width), BF16),
        ],
        scratch_shapes=[
            pltpu.VMEM((parts, rows, width), F32),
            pltpu.VMEM((parts, rows, width), F32),
            pltpu.VMEM((parts, rows, width), F32),
            pltpu.VMEM((parts, rows, width), BF16),
            pltpu.VMEM((parts, rows, width), F32),
            pltpu.VMEM((parts, rows, width), BF16),
            pltpu.SemaphoreType.DMA((parts, 4)),
            pltpu.SemaphoreType.DMA((parts, 2)),
        ],
        compiler_params=pltpu.CompilerParams(vmem_limit_bytes=60 * MIB),
        cost_estimate=pl.CostEstimate(
            flops=12 * rows * columns, bytes_accessed=20 * rows * columns, transcendentals=0
        ),
        name="adam",
    )(master, moment, second, grad)


def offset(i):
    total = 0
    for k, hop in enumerate(HOPS):
        if i >> (len(HOPS) - 1 - k) & 1:
            total ^= hop
    return total


def stage_kernel(lengths, versions, recorded, hidden, meta, spread):
    rows, steps = recorded.shape
    lane = lax.broadcasted_iota(jnp.int32, (1, 128), 1)
    line = jnp.zeros((1, 128), F32)
    for r in range(rows):
        for s in range(steps):
            at = r * steps + s
            line = jnp.where(lane == rows * steps + at, recorded[r, s], line)
            line = jnp.where(lane == 2 * rows * steps + at, versions[r].astype(F32), line)
    meta[0:1] = line
    for r in range(rows):
        meta[r + 1 : r + 2] = jnp.full((1, 128), lengths[r].astype(F32))
    me = lax.axis_index("fsdp")
    depth = spread.shape[2]
    for f in range(spread.shape[0]):
        at = pl.ds(pl.multiple_of((me ^ offset(f)) * depth, depth), depth)
        for r in range(rows):
            spread[f, r * steps : (r + 1) * steps] = hidden[r, :, at]


def stage(lengths, versions, recorded, hidden, n_fsdp):
    rows, steps, width = hidden.shape
    return pl.pallas_call(
        stage_kernel,
        in_specs=[SMEM, SMEM, SMEM, VMEM],
        out_specs=[VMEM] * 2,
        out_shape=[
            jax.ShapeDtypeStruct((8, 128), F32),
            jax.ShapeDtypeStruct((n_fsdp, rows * steps, width // n_fsdp), BF16),
        ],
        compiler_params=pltpu.CompilerParams(vmem_limit_bytes=16 * MIB),
        name="stage",
    )(in_hbm(lengths), in_hbm(versions), in_hbm(recorded), in_hbm(hidden))


def product_kernel(flip, spread, weights, out):
    me = lax.axis_index("fsdp")
    chips = out.shape[0] // spread.shape[1]
    where = {offset(i): i for i in range(spread.shape[0])}
    blocks = []
    for chip in range(chips):
        away = me ^ flip ^ (2 * chip + (me & 1))
        at = jnp.int32(0)
        for far, i in where.items():
            at = jnp.where(away == far, i, at)
        blocks.append(spread[at])
    out[...] = jnp.dot(
        jnp.concatenate(blocks, axis=0), weights[...], preferred_element_type=F32
    )


def product(spread, weights, n_fsdp, flip):
    _, tall, depth = spread.shape
    width = weights.shape[1]
    return pl.pallas_call(
        functools.partial(product_kernel, flip),
        in_specs=[VMEM] * 2,
        out_specs=VMEM,
        out_shape=jax.ShapeDtypeStruct((n_fsdp // 2 * tall, width), F32),
        compiler_params=pltpu.CompilerParams(vmem_limit_bytes=16 * MIB),
        cost_estimate=pl.CostEstimate(
            flops=n_fsdp * tall * depth * width, bytes_accessed=16 * MIB, transcendentals=0
        ),
        name="product",
    )(spread, weights)


def score_kernel(steps, parts, cache, meta, probs, base, lse_out):
    rows = cache.shape[0]
    heads = parts.shape[2] // HD - 2
    total = parts[0]
    for i in range(1, parts.shape[0]):
        total = total + parts[i]
    scale = HD ** (-0.5)
    contract = (((1,), (1,)), ((), ()))
    line = meta[0:1]
    for r in range(rows):
        mine = total[r * steps : (r + 1) * steps]
        queries = jnp.concatenate(
            [mine[:, h * HD : (h + 1) * HD] for h in range(heads)], axis=0
        ).astype(BF16)
        new_keys = mine[:, heads * HD : (heads + 1) * HD].astype(BF16)
        new_values = mine[:, (heads + 1) * HD :].astype(BF16)
        old = lax.dot_general(queries, cache[r, 0, 0], contract, preferred_element_type=F32)
        slot = lax.broadcasted_iota(jnp.int32, old.shape, 1).astype(F32)
        old = jnp.where(slot < meta[r + 1 : r + 2, 0:1], old, -1e31)
        new = lax.dot_general(queries, new_keys, contract, preferred_element_type=F32)
        step = lax.broadcasted_iota(jnp.int32, new.shape, 0) % steps
        later = lax.broadcasted_iota(jnp.int32, new.shape, 1)
        new = jnp.where(later <= step, new, -1e31)
        top = jnp.maximum(
            jnp.max(old, axis=1, keepdims=True), jnp.max(new, axis=1, keepdims=True)
        )
        old = jnp.exp2((old - top) * (scale * LOG2E))
        new = jnp.exp2((new - top) * (scale * LOG2E))
        mass = jnp.sum(old, axis=1, keepdims=True) + jnp.sum(new, axis=1, keepdims=True)
        lse = top * scale + jnp.log(mass)
        inverse = 1.0 / mass
        probs[r] = (old * inverse).astype(BF16)
        base[r] = jnp.dot((new * inverse).astype(BF16), new_values, preferred_element_type=F32)
        place = lax.broadcasted_iota(jnp.int32, (heads * steps, 128), 0) % steps + r * steps
        lane = lax.broadcasted_iota(jnp.int32, (heads * steps, 128), 1)
        line = line + jnp.sum(jnp.where(place == lane, lse, 0.0), axis=0, keepdims=True)
    lse_out[...] = jnp.broadcast_to(line, lse_out.shape)


def score(parts, cache, meta, steps, copies):
    rows, _, _, slots, _ = cache.shape
    heads = parts.shape[2] // HD - 2
    return pl.pallas_call(
        functools.partial(score_kernel, steps),
        in_specs=[VMEM] * 3,
        out_specs=[VMEM] * 3,
        out_shape=[
            jax.ShapeDtypeStruct((rows, heads * steps, slots), BF16),
            jax.ShapeDtypeStruct((rows, heads * steps, HD), F32),
            jax.ShapeDtypeStruct((copies, 128), F32),
        ],
        compiler_params=pltpu.CompilerParams(vmem_limit_bytes=24 * MIB),
        cost_estimate=pl.CostEstimate(
            flops=2 * rows * heads * steps * slots * HD,
            bytes_accessed=cache.size,
            transcendentals=rows * heads * steps * slots,
        ),
        name="score",
    )(parts, in_vmem(cache), meta)


def mix_kernel(steps, probs, base, values, out):
    tall = probs.shape[1]
    mixed = jnp.dot(probs[0], values[0, 0, 0], preferred_element_type=F32) + base[0]
    mixed = mixed.astype(BF16)
    out[0] = jnp.concatenate(
        [mixed[h * steps : (h + 1) * steps] for h in range(tall // steps)], axis=1
    )


def mix(probs, base, cache, steps):
    rows, tall, slots = probs.shape
    width = tall // steps * HD
    return pl.pallas_call(
        functools.partial(mix_kernel, steps),
        grid=(rows,),
        in_specs=[
            pl.BlockSpec((1, tall, slots), lambda r: (r, 0, 0)),
            pl.BlockSpec((1, tall, HD), lambda r: (r, 0, 0)),
            pl.BlockSpec((1, 1, 1, slots, HD), lambda r: (r, 0, 1, 0, 0)),
        ],
        out_specs=pl.BlockSpec((1, steps, width), lambda r: (r, 0, 0)),
        out_shape=jax.ShapeDtypeStruct((rows, steps, width), BF16),
        compiler_params=pltpu.CompilerParams(vmem_limit_bytes=24 * MIB),
        cost_estimate=pl.CostEstimate(
            flops=2 * rows * tall * slots * HD, bytes_accessed=cache.size, transcendentals=0
        ),
        name="mix",
    )(probs, base, in_hbm(cache))


def ratio_kernel(gathered, ratios, means):
    rows, steps = ratios.shape
    count = rows * steps
    n_fsdp = lax.axis_size("fsdp")
    n_tp = gathered.shape[0] // n_fsdp
    lines = gathered[...].reshape(n_fsdp, n_tp, 128)
    normalizer = jnp.sum(lines, axis=1)[:, :count] / H
    first = lines[:, 0]
    recorded = first[:, count : 2 * count]
    version = first[:, 2 * count : 3 * count]
    ratio = jnp.exp(jnp.clip(normalizer - recorded, -2.0, 2.0))
    for v in range(VERSIONS):
        hit = version == float(v)
        members = jnp.sum(jnp.where(hit, 1.0, 0.0))
        means[v] = jnp.sum(jnp.where(hit, ratio, 0.0)) / jnp.maximum(members, 1.0)
    group = lax.broadcasted_iota(jnp.int32, ratio.shape, 0)
    mine = jnp.sum(
        jnp.where(group == lax.axis_index("fsdp"), ratio, 0.0), axis=0, keepdims=True
    )
    for r in range(rows):
        ratios[r : r + 1] = mine[:, r * steps : (r + 1) * steps]


def final(gathered, rows, steps):
    return pl.pallas_call(
        ratio_kernel,
        in_specs=[VMEM],
        out_specs=[VMEM, SMEM],
        out_shape=[
            jax.ShapeDtypeStruct((rows, steps), F32),
            jax.ShapeDtypeStruct((VERSIONS,), F32),
        ],
        name="ratios",
    )(in_vmem(gathered))


def shards(master, moment, second, grad, hidden, cache, lengths, recorded, versions):
    n_tp = lax.axis_size("tp")
    n_fsdp = lax.axis_size("fsdp")
    rows, steps, width = hidden.shape
    tall = rows * steps
    depth = width // n_fsdp
    chips = n_fsdp // 2
    cores = [[i for i in range(n_fsdp) if i % 2 == c] for c in range(2)]
    pairs = [(i, i ^ 1) for i in range(n_fsdp)]

    meta, spread = stage(lengths, versions, recorded, hidden, n_fsdp)
    new_master, fresh = adam(master, moment, second, grad, n_tp)
    for k, hop in enumerate(HOPS):
        halves = spread.reshape(2**k, 2, -1, tall, depth)
        moved = lax.ppermute(halves[:, 1], "fsdp", [(i, i ^ hop) for i in range(n_fsdp)])
        if k == 0:
            moved, fresh = lax.optimization_barrier((moved, fresh))
        spread = jnp.stack([halves[:, 0], moved], axis=1)
    spread = spread.reshape(n_fsdp, tall, depth)
    weights = lax.all_to_all(fresh, "tp", 0, 0, tiled=True).reshape(depth, -1)

    sent = product(spread, weights, n_fsdp, 1)
    arrived = lax.ppermute(sent, "fsdp", pairs)
    partial = product(spread, weights, n_fsdp, 0) + arrived
    parts = lax.all_to_all(
        partial.reshape(chips, tall, -1), "fsdp", 0, 0, tiled=True, axis_index_groups=cores
    )
    probs, base, lines = score(parts, cache, meta, steps, n_fsdp * n_tp)
    lines = lax.all_to_all(lines, ("fsdp", "tp"), 0, 0, tiled=True)
    attention = mix(probs, base, cache, steps)
    ratios, version_means = final(lines, rows, steps)
    return (new_master, attention, ratios, version_means)


def solution(mesh):
    in_specs = (
        P(("fsdp", "tp"), None),
        P(("fsdp", "tp"), None),
        P(("fsdp", "tp"), None),
        P(("fsdp", "tp"), None),
        P("fsdp", None, None),
        P("fsdp", "tp", None, None, None),
        P("fsdp"),
        P("fsdp", None),
        P("fsdp"),
    )
    out_specs = (P(("fsdp", "tp"), None), P("fsdp", None, "tp"), P("fsdp", None), P())
    return jax.shard_map(shards, mesh=mesh, in_specs=in_specs, out_specs=out_specs, check_vma=False)
```

```python
import functools

import jax
import jax.numpy as jnp
from jax import lax
from jax.experimental import pallas as pl
from jax.experimental.pallas import tpu as pltpu
from jax.sharding import PartitionSpec as P

H = 64
HD = 128
VERSIONS = 4
F32 = jnp.float32
BF16 = jnp.bfloat16
ANY = pl.BlockSpec(memory_space=pl.ANY)
VMEM = pl.BlockSpec(memory_space=pltpu.VMEM)
SMEM = pl.BlockSpec(memory_space=pltpu.SMEM)
MIB = 1 << 20
in_hbm = functools.partial(pltpu.with_memory_space_constraint, memory_space=pltpu.HBM)
in_vmem = functools.partial(pltpu.with_memory_space_constraint, memory_space=pltpu.VMEM)
LOG2E = 1.4426950408889634
AHEAD = 3
HOPS = ((0, 8), (0, 2, 4, 6), (0, 1))


def adam_kernel(master, moment, second, grad, out, a, b, c, g, n, arrive, leave):
    parts, rows, width = n.shape
    sources = ((master, a), (moment, b), (second, c), (grad, g))

    def columns(i):
        return pl.ds(i * width, width)

    def fetches(i):
        return [
            pltpu.make_async_copy(hbm.at[:, columns(i)], buf.at[i], arrive.at[i, k])
            for k, (hbm, buf) in enumerate(sources)
        ]

    def store(i):
        to = out.at[i] if len(out.shape) == 3 else out.at[:, columns(i)]
        return pltpu.make_async_copy(n.at[i], to, leave.at[i])

    for i in range(AHEAD):
        for copy in fetches(i):
            copy.start()
    for i in range(parts):
        if i + AHEAD < parts:
            for copy in fetches(i + AHEAD):
                copy.start()
        for copy in fetches(i):
            copy.wait()

        def tile(k, carry, i=i):
            at = pl.ds(pl.multiple_of(k * 16, 16), 16)
            gradient = g[i, at].astype(F32)
            fresh_moment = 0.9 * b[i, at] + 0.1 * gradient
            fresh_second = 0.95 * c[i, at] + 0.05 * gradient * gradient
            spread = jnp.sqrt(fresh_second * (1.0 / (1.0 - 0.95**10))) + 1e-08
            fresh = a[i, at] - (0.005 / (1.0 - 0.9**10)) * fresh_moment / spread
            n[i, at] = fresh.astype(n.dtype)
            return carry

        lax.fori_loop(0, rows // 16, tile, 0)
        store(i).start()
    for i in range(parts):
        store(i).wait()


def adam(arrays, parts, shape, kind, name):
    rows, columns = arrays[0].shape
    width = columns // parts
    kinds = [x.dtype for x in arrays] + [kind]
    return pl.pallas_call(
        adam_kernel,
        in_specs=[ANY] * 4,
        out_specs=ANY,
        out_shape=jax.ShapeDtypeStruct(shape, kind),
        scratch_shapes=[
            *(pltpu.VMEM((parts, rows, width), k) for k in kinds),
            pltpu.SemaphoreType.DMA((parts, 4)),
            pltpu.SemaphoreType.DMA((parts,)),
        ],
        compiler_params=pltpu.CompilerParams(vmem_limit_bytes=60 * MIB),
        cost_estimate=pl.CostEstimate(
            flops=12 * rows * columns, bytes_accessed=18 * rows * columns, transcendentals=0
        ),
        name=name,
    )(*arrays)


def offset(i):
    total = 0
    for hops in reversed(HOPS):
        total ^= hops[i % len(hops)]
        i //= len(hops)
    return total


def stage_kernel(lengths, versions, recorded, hidden, meta, spread):
    rows, steps = recorded.shape
    lane = lax.broadcasted_iota(jnp.int32, (1, 128), 1)
    line = jnp.zeros((1, 128), F32)
    for r in range(rows):
        for s in range(steps):
            at = r * steps + s
            line = jnp.where(lane == rows * steps + at, recorded[r, s], line)
            line = jnp.where(lane == 2 * rows * steps + at, versions[r].astype(F32), line)
    meta[0:1] = line
    for r in range(rows):
        meta[r + 1 : r + 2] = jnp.full((1, 128), lengths[r].astype(F32))
    me = lax.axis_index("fsdp")
    depth = spread.shape[2]
    for f in range(spread.shape[0]):
        at = pl.ds(pl.multiple_of((me ^ offset(f)) * depth, depth), depth)
        for r in range(rows):
            spread[f, r * steps : (r + 1) * steps] = hidden[r, :, at]


def stage(lengths, versions, recorded, hidden, n_fsdp):
    rows, steps, width = hidden.shape
    return pl.pallas_call(
        stage_kernel,
        in_specs=[SMEM, SMEM, SMEM, VMEM],
        out_specs=[VMEM] * 2,
        out_shape=[
            jax.ShapeDtypeStruct((8, 128), F32),
            jax.ShapeDtypeStruct((n_fsdp, rows * steps, width // n_fsdp), BF16),
        ],
        compiler_params=pltpu.CompilerParams(vmem_limit_bytes=16 * MIB),
        name="stage",
    )(in_hbm(lengths), in_hbm(versions), in_hbm(recorded), in_hbm(hidden))


def product_kernel(flip, spread, weights, *rest):
    keys = None
    if flip:
        _, out = rest
    else:
        cache, out, keys, sems = rest
        copies = [
            pltpu.make_async_copy(cache.at[r, 0, 0], keys.at[r], sems.at[r])
            for r in range(keys.shape[0])
        ]
        for copy in copies:
            copy.start()
    me = lax.axis_index("fsdp")
    chips = out.shape[0] // spread.shape[1]
    blocks = []
    for chip in range(chips):
        away = me ^ flip ^ (2 * chip + (me & 1))
        at = jnp.int32(0)
        for i in range(spread.shape[0]):
            at = jnp.where(away == offset(i), i, at)
        blocks.append(spread[at])
    out[...] = jnp.dot(
        jnp.concatenate(blocks, axis=0), weights[...], preferred_element_type=F32
    )
    if not flip:
        for copy in copies:
            copy.wait()


def product(spread, weights, n_fsdp, flip, after=None, cache=None):
    _, tall, depth = spread.shape
    width = weights.shape[1]
    partial = jax.ShapeDtypeStruct((n_fsdp // 2 * tall, width), F32)
    if flip:
        extra = dict(in_specs=[VMEM] * 2 + [ANY], out_specs=VMEM, out_shape=partial)
        operands = (in_hbm(after),)
    else:
        rows, _, _, slots, _ = cache.shape
        extra = dict(
            in_specs=[VMEM] * 2 + [ANY],
            out_specs=[VMEM] * 2,
            out_shape=[partial, pltpu.VMEM((rows, slots, HD), BF16)],
            scratch_shapes=[pltpu.SemaphoreType.DMA((rows,))],
        )
        operands = (in_hbm(cache),)
    return pl.pallas_call(
        functools.partial(product_kernel, flip),
        compiler_params=pltpu.CompilerParams(vmem_limit_bytes=16 * MIB),
        cost_estimate=pl.CostEstimate(
            flops=n_fsdp * tall * depth * width, bytes_accessed=2 * MIB, transcendentals=0
        ),
        name="product",
        **extra,
    )(spread, weights, *operands)


def score_kernel(steps, parts, keys, meta, probs, base, lse_out):
    rows = keys.shape[0]
    heads = parts.shape[2] // HD - 2
    total = parts[0]
    for i in range(1, parts.shape[0]):
        total = total + parts[i]
    scale = HD ** (-0.5)
    contract = (((1,), (1,)), ((), ()))
    line = meta[0:1]
    for r in range(rows):
        mine = total[r * steps : (r + 1) * steps]
        queries = jnp.concatenate(
            [mine[:, h * HD : (h + 1) * HD] for h in range(heads)], axis=0
        ).astype(BF16)
        new_keys = mine[:, heads * HD : (heads + 1) * HD].astype(BF16)
        new_values = mine[:, (heads + 1) * HD :].astype(BF16)
        old = lax.dot_general(queries, keys[r], contract, preferred_element_type=F32)
        slot = lax.broadcasted_iota(jnp.int32, old.shape, 1).astype(F32)
        old = jnp.where(slot < meta[r + 1 : r + 2, 0:1], old, -1e31)
        new = lax.dot_general(queries, new_keys, contract, preferred_element_type=F32)
        step = lax.broadcasted_iota(jnp.int32, new.shape, 0) % steps
        later = lax.broadcasted_iota(jnp.int32, new.shape, 1)
        new = jnp.where(later <= step, new, -1e31)
        top = jnp.maximum(
            jnp.max(old, axis=1, keepdims=True), jnp.max(new, axis=1, keepdims=True)
        )
        old = jnp.exp2((old - top) * (scale * LOG2E))
        new = jnp.exp2((new - top) * (scale * LOG2E))
        mass = jnp.sum(old, axis=1, keepdims=True) + jnp.sum(new, axis=1, keepdims=True)
        lse = top * scale + jnp.log(mass)
        inverse = 1.0 / mass
        probs[r] = (old * inverse).astype(BF16)
        base[r] = jnp.dot((new * inverse).astype(BF16), new_values, preferred_element_type=F32)
        place = lax.broadcasted_iota(jnp.int32, (heads * steps, 128), 0) % steps + r * steps
        lane = lax.broadcasted_iota(jnp.int32, (heads * steps, 128), 1)
        line = line + jnp.sum(jnp.where(place == lane, lse, 0.0), axis=0, keepdims=True)
    lse_out[...] = jnp.broadcast_to(line, lse_out.shape)


def score(parts, keys, meta, steps, copies):
    rows, slots, _ = keys.shape
    heads = parts.shape[2] // HD - 2
    return pl.pallas_call(
        functools.partial(score_kernel, steps),
        in_specs=[VMEM] * 3,
        out_specs=[VMEM] * 3,
        out_shape=[
            jax.ShapeDtypeStruct((rows, heads * steps, slots), BF16),
            jax.ShapeDtypeStruct((rows, heads * steps, HD), F32),
            jax.ShapeDtypeStruct((copies, 128), F32),
        ],
        compiler_params=pltpu.CompilerParams(vmem_limit_bytes=24 * MIB),
        cost_estimate=pl.CostEstimate(
            flops=2 * rows * heads * steps * slots * HD,
            bytes_accessed=2 * keys.size,
            transcendentals=rows * heads * steps * slots,
        ),
        name="score",
    )(parts, in_vmem(keys), meta)


def mix_kernel(steps, probs, base, values, out):
    tall = probs.shape[1]
    mixed = jnp.dot(probs[0], values[0, 0, 0], preferred_element_type=F32) + base[0]
    mixed = mixed.astype(BF16)
    out[0] = jnp.concatenate(
        [mixed[h * steps : (h + 1) * steps] for h in range(tall // steps)], axis=1
    )


def mix(probs, base, cache, steps):
    rows, tall, slots = probs.shape
    width = tall // steps * HD
    return pl.pallas_call(
        functools.partial(mix_kernel, steps),
        grid=(rows,),
        in_specs=[
            pl.BlockSpec((1, tall, slots), lambda r: (r, 0, 0)),
            pl.BlockSpec((1, tall, HD), lambda r: (r, 0, 0)),
            pl.BlockSpec((1, 1, 1, slots, HD), lambda r: (r, 0, 1, 0, 0)),
        ],
        out_specs=pl.BlockSpec((1, steps, width), lambda r: (r, 0, 0)),
        out_shape=jax.ShapeDtypeStruct((rows, steps, width), BF16),
        compiler_params=pltpu.CompilerParams(vmem_limit_bytes=24 * MIB),
        cost_estimate=pl.CostEstimate(
            flops=2 * rows * tall * slots * HD, bytes_accessed=cache.size, transcendentals=0
        ),
        name="mix",
    )(probs, base, in_hbm(cache))


def ratio_kernel(gathered, ratios, means):
    rows, steps = ratios.shape
    count = rows * steps
    n_fsdp = lax.axis_size("fsdp")
    n_tp = gathered.shape[0] // n_fsdp
    lines = gathered[...].reshape(n_fsdp, n_tp, 128)
    normalizer = jnp.sum(lines, axis=1)[:, :count] / H
    first = lines[:, 0]
    recorded = first[:, count : 2 * count]
    version = first[:, 2 * count : 3 * count]
    ratio = jnp.exp(jnp.clip(normalizer - recorded, -2.0, 2.0))
    for v in range(VERSIONS):
        hit = version == float(v)
        members = jnp.sum(jnp.where(hit, 1.0, 0.0))
        means[v] = jnp.sum(jnp.where(hit, ratio, 0.0)) / jnp.maximum(members, 1.0)
    group = lax.broadcasted_iota(jnp.int32, ratio.shape, 0)
    mine = jnp.sum(
        jnp.where(group == lax.axis_index("fsdp"), ratio, 0.0), axis=0, keepdims=True
    )
    for r in range(rows):
        ratios[r : r + 1] = mine[:, r * steps : (r + 1) * steps]


def final(gathered, rows, steps):
    return pl.pallas_call(
        ratio_kernel,
        in_specs=[VMEM],
        out_specs=[VMEM, SMEM],
        out_shape=[
            jax.ShapeDtypeStruct((rows, steps), F32),
            jax.ShapeDtypeStruct((VERSIONS,), F32),
        ],
        name="ratios",
    )(in_vmem(gathered))


def shards(master, moment, second, grad, hidden, cache, lengths, recorded, versions):
    n_tp = lax.axis_size("tp")
    n_fsdp = lax.axis_size("fsdp")
    rows, steps, width = hidden.shape
    tall = rows * steps
    depth = width // n_fsdp
    chips = n_fsdp // 2
    cores = [[i for i in range(n_fsdp) if i % 2 == c] for c in range(2)]

    def move(block, hop):
        return lax.ppermute(block, "fsdp", [(i, i ^ hop) for i in range(n_fsdp)]) if hop else block

    meta, spread = stage(lengths, versions, recorded, hidden, n_fsdp)
    spread = spread.reshape(*(len(hops) for hops in HOPS), tall, depth)
    along_x = [move(spread[k], hop) for k, hop in enumerate(HOPS[0])]

    learned = (master, moment, second, grad)
    fresh = adam(learned, n_tp, (n_tp, master.shape[0], master.shape[1] // n_tp), BF16, "weights")
    fresh, along_x, learned = lax.optimization_barrier((fresh, along_x, learned))
    weights = lax.all_to_all(fresh, "tp", 0, 0, tiled=True).reshape(depth, -1)
    new_master = adam(learned, n_tp, master.shape, F32, "master")

    spread = jnp.stack(along_x)
    spread = jnp.stack([move(spread[:, k], hop) for k, hop in enumerate(HOPS[1])], axis=1)
    spread = jnp.stack([move(spread[:, :, k], hop) for k, hop in enumerate(HOPS[2])], axis=2)
    spread = spread.reshape(n_fsdp, tall, depth)

    sent = product(spread, weights, n_fsdp, 1, after=new_master)
    arrived = move(sent, 1)
    partial, keys = product(spread, weights, n_fsdp, 0, cache=cache)
    partial = partial + arrived
    parts = lax.all_to_all(
        partial.reshape(chips, tall, -1), "fsdp", 0, 0, tiled=True, axis_index_groups=cores
    )
    probs, base, lines = score(parts, keys, meta, steps, n_fsdp * n_tp)
    lines = lax.all_to_all(lines, ("fsdp", "tp"), 0, 0, tiled=True)
    attention = mix(probs, base, cache, steps)
    ratios, version_means = final(lines, rows, steps)
    return (new_master, attention, ratios, version_means)


def solution(mesh):
    in_specs = (
        P(("fsdp", "tp"), None),
        P(("fsdp", "tp"), None),
        P(("fsdp", "tp"), None),
        P(("fsdp", "tp"), None),
        P("fsdp", None, None),
        P("fsdp", "tp", None, None, None),
        P("fsdp"),
        P("fsdp", None),
        P("fsdp"),
    )
    out_specs = (P(("fsdp", "tp"), None), P("fsdp", None, "tp"), P("fsdp", None), P())
    return jax.shard_map(shards, mesh=mesh, in_specs=in_specs, out_specs=out_specs, check_vma=False)
```

```python
import functools

import jax
import jax.numpy as jnp
from jax import lax
from jax.experimental import pallas as pl
from jax.experimental.pallas import tpu as pltpu
from jax.sharding import PartitionSpec as P

H = 64
HD = 128
VERSIONS = 4
F32 = jnp.float32
BF16 = jnp.bfloat16
ANY = pl.BlockSpec(memory_space=pl.ANY)
VMEM = pl.BlockSpec(memory_space=pltpu.VMEM)
SMEM = pl.BlockSpec(memory_space=pltpu.SMEM)
MIB = 1 << 20
in_hbm = functools.partial(pltpu.with_memory_space_constraint, memory_space=pltpu.HBM)
in_vmem = functools.partial(pltpu.with_memory_space_constraint, memory_space=pltpu.VMEM)
LOG2E = 1.4426950408889634
AHEAD = 8
HOPS = ((0, 8), (0, 2, 4, 6), (0, 1))


def adam_kernel(master, moment, second, grad, out, a, b, c, g, n, arrive, leave):
    parts, rows, width = n.shape
    sources = ((master, a), (moment, b), (second, c), (grad, g))

    def columns(i):
        return pl.ds(i * width, width)

    def fetches(i):
        return [
            pltpu.make_async_copy(hbm.at[:, columns(i)], buf.at[i], arrive.at[i, k])
            for k, (hbm, buf) in enumerate(sources)
        ]

    def store(i):
        to = out.at[i] if len(out.shape) == 3 else out.at[:, columns(i)]
        return pltpu.make_async_copy(n.at[i], to, leave.at[i])

    for i in range(AHEAD):
        for copy in fetches(i):
            copy.start()
    for i in range(parts):
        if i + AHEAD < parts:
            for copy in fetches(i + AHEAD):
                copy.start()
        for copy in fetches(i):
            copy.wait()

        def tile(k, carry, i=i):
            at = pl.ds(pl.multiple_of(k * 16, 16), 16)
            gradient = g[i, at].astype(F32)
            fresh_moment = 0.9 * b[i, at] + 0.1 * gradient
            fresh_second = 0.95 * c[i, at] + 0.05 * gradient * gradient
            spread = jnp.sqrt(fresh_second * (1.0 / (1.0 - 0.95**10))) + 1e-08
            fresh = a[i, at] - (0.005 / (1.0 - 0.9**10)) * fresh_moment / spread
            n[i, at] = fresh.astype(n.dtype)
            return carry

        lax.fori_loop(0, rows // 16, tile, 0)
        store(i).start()
    for i in range(parts):
        store(i).wait()


def adam(arrays, parts, shape, kind, name):
    rows, columns = arrays[0].shape
    width = columns // parts
    kinds = [x.dtype for x in arrays] + [kind]
    return pl.pallas_call(
        adam_kernel,
        in_specs=[ANY] * 4,
        out_specs=ANY,
        out_shape=jax.ShapeDtypeStruct(shape, kind),
        scratch_shapes=[
            *(pltpu.VMEM((parts, rows, width), k) for k in kinds),
            pltpu.SemaphoreType.DMA((parts, 4)),
            pltpu.SemaphoreType.DMA((parts,)),
        ],
        compiler_params=pltpu.CompilerParams(vmem_limit_bytes=60 * MIB),
        cost_estimate=pl.CostEstimate(
            flops=12 * rows * columns, bytes_accessed=18 * rows * columns, transcendentals=0
        ),
        name=name,
    )(*arrays)


def offset(i):
    total = 0
    for hops in reversed(HOPS):
        total ^= hops[i % len(hops)]
        i //= len(hops)
    return total


def stage_kernel(lengths, versions, recorded, hidden, meta, spread):
    rows, steps = recorded.shape
    lane = lax.broadcasted_iota(jnp.int32, (1, 128), 1)
    line = jnp.zeros((1, 128), F32)
    for r in range(rows):
        for s in range(steps):
            at = r * steps + s
            line = jnp.where(lane == rows * steps + at, recorded[r, s], line)
            line = jnp.where(lane == 2 * rows * steps + at, versions[r].astype(F32), line)
    meta[0:1] = line
    for r in range(rows):
        meta[r + 1 : r + 2] = jnp.full((1, 128), lengths[r].astype(F32))
    me = lax.axis_index("fsdp")
    depth = spread.shape[2]
    for f in range(spread.shape[0]):
        at = pl.ds(pl.multiple_of((me ^ offset(f)) * depth, depth), depth)
        for r in range(rows):
            spread[f, r * steps : (r + 1) * steps] = hidden[r, :, at]


def stage(lengths, versions, recorded, hidden, n_fsdp):
    rows, steps, width = hidden.shape
    return pl.pallas_call(
        stage_kernel,
        in_specs=[SMEM, SMEM, SMEM, VMEM],
        out_specs=[VMEM] * 2,
        out_shape=[
            jax.ShapeDtypeStruct((8, 128), F32),
            jax.ShapeDtypeStruct((n_fsdp, rows * steps, width // n_fsdp), BF16),
        ],
        compiler_params=pltpu.CompilerParams(vmem_limit_bytes=16 * MIB),
        name="stage",
    )(in_hbm(lengths), in_hbm(versions), in_hbm(recorded), in_hbm(hidden))


def product_kernel(flip, spread, weights, *rest):
    keys = None
    if flip:
        (out,) = rest
    else:
        cache, out, keys, sems = rest
        copies = [
            pltpu.make_async_copy(cache.at[r, 0, 0], keys.at[r], sems.at[r])
            for r in range(keys.shape[0])
        ]
        for copy in copies:
            copy.start()
    me = lax.axis_index("fsdp")
    chips = out.shape[0] // spread.shape[1]
    blocks = []
    for chip in range(chips):
        away = me ^ flip ^ (2 * chip + (me & 1))
        at = jnp.int32(0)
        for i in range(spread.shape[0]):
            at = jnp.where(away == offset(i), i, at)
        blocks.append(spread[at])
    out[...] = jnp.dot(
        jnp.concatenate(blocks, axis=0), weights[...], preferred_element_type=F32
    )
    if not flip:
        for copy in copies:
            copy.wait()


def product(spread, weights, n_fsdp, flip, cache=None):
    _, tall, depth = spread.shape
    width = weights.shape[1]
    partial = jax.ShapeDtypeStruct((n_fsdp // 2 * tall, width), F32)
    if flip:
        extra = dict(in_specs=[VMEM] * 2, out_specs=VMEM, out_shape=partial)
        operands = ()
    else:
        rows, _, _, slots, _ = cache.shape
        extra = dict(
            in_specs=[VMEM] * 2 + [ANY],
            out_specs=[VMEM] * 2,
            out_shape=[partial, pltpu.VMEM((rows - 1, slots, HD), BF16)],
            scratch_shapes=[pltpu.SemaphoreType.DMA((rows - 1,))],
        )
        operands = (in_hbm(cache),)
    return pl.pallas_call(
        functools.partial(product_kernel, flip),
        compiler_params=pltpu.CompilerParams(vmem_limit_bytes=16 * MIB),
        cost_estimate=pl.CostEstimate(
            flops=n_fsdp * tall * depth * width, bytes_accessed=2 * MIB, transcendentals=0
        ),
        name="product",
        **extra,
    )(spread, weights, *operands)


def score_kernel(steps, parts, keys, cache, meta, probs, base, lse_out, last, p, arrive, leave):
    rows = cache.shape[0]
    heads = parts.shape[2] // HD - 2
    fetch = pltpu.make_async_copy(cache.at[rows - 1, 0, 0], last, arrive)
    fetch.start()
    total = parts[0]
    for i in range(1, parts.shape[0]):
        total = total + parts[i]
    scale = HD ** (-0.5)
    contract = (((1,), (1,)), ((), ()))

    def scores(r):
        mine = total[r * steps : (r + 1) * steps]
        queries = jnp.concatenate(
            [mine[:, h * HD : (h + 1) * HD] for h in range(heads)], axis=0
        ).astype(BF16)
        new_keys = mine[:, heads * HD : (heads + 1) * HD].astype(BF16)
        new_values = mine[:, (heads + 1) * HD :].astype(BF16)
        if r == rows - 1:
            fetch.wait()
        old_keys = last[...] if r == rows - 1 else keys[r]
        old = lax.dot_general(queries, old_keys, contract, preferred_element_type=F32)
        slot = lax.broadcasted_iota(jnp.int32, old.shape, 1).astype(F32)
        old = jnp.where(slot < meta[r + 1 : r + 2, 0:1], old, -1e31)
        new = lax.dot_general(queries, new_keys, contract, preferred_element_type=F32)
        step = lax.broadcasted_iota(jnp.int32, new.shape, 0) % steps
        later = lax.broadcasted_iota(jnp.int32, new.shape, 1)
        return old, jnp.where(later <= step, new, -1e31), new_values

    def store(r):
        return pltpu.make_async_copy(p.at[r], probs.at[r], leave.at[r])

    line = meta[0:1]
    following = scores(0)
    for r in range(rows):
        old, new, new_values = following
        if r + 1 < rows:
            following = scores(r + 1)
        top = jnp.maximum(
            jnp.max(old, axis=1, keepdims=True), jnp.max(new, axis=1, keepdims=True)
        )
        old = jnp.exp2((old - top) * (scale * LOG2E))
        new = jnp.exp2((new - top) * (scale * LOG2E))
        mass = jnp.sum(old, axis=1, keepdims=True) + jnp.sum(new, axis=1, keepdims=True)
        lse = top * scale + jnp.log(mass)
        inverse = 1.0 / mass
        p[r] = (old * inverse).astype(BF16)
        store(r).start()
        base[r] = jnp.dot((new * inverse).astype(BF16), new_values, preferred_element_type=F32)
        place = lax.broadcasted_iota(jnp.int32, (heads * steps, 128), 0) % steps + r * steps
        lane = lax.broadcasted_iota(jnp.int32, (heads * steps, 128), 1)
        line = line + jnp.sum(jnp.where(place == lane, lse, 0.0), axis=0, keepdims=True)
    lse_out[...] = jnp.broadcast_to(line, lse_out.shape)
    for r in range(rows):
        store(r).wait()


def score(parts, keys, cache, meta, copies):
    rows, _, _, slots, _ = cache.shape
    heads = parts.shape[2] // HD - 2
    steps = parts.shape[1] // rows
    return pl.pallas_call(
        functools.partial(score_kernel, steps),
        in_specs=[VMEM, VMEM, ANY, VMEM],
        out_specs=[ANY, VMEM, VMEM],
        out_shape=[
            jax.ShapeDtypeStruct((rows, heads * steps, slots), BF16),
            jax.ShapeDtypeStruct((rows, heads * steps, HD), F32),
            jax.ShapeDtypeStruct((copies, 128), F32),
        ],
        scratch_shapes=[
            pltpu.VMEM((slots, HD), BF16),
            pltpu.VMEM((rows, heads * steps, slots), BF16),
            pltpu.SemaphoreType.DMA,
            pltpu.SemaphoreType.DMA((rows,)),
        ],
        compiler_params=pltpu.CompilerParams(vmem_limit_bytes=24 * MIB),
        cost_estimate=pl.CostEstimate(
            flops=2 * rows * heads * steps * slots * HD,
            bytes_accessed=cache.size,
            transcendentals=rows * heads * steps * slots,
        ),
        name="score",
    )(parts, in_vmem(keys), in_hbm(cache), meta)


def mix_kernel(steps, probs, base, values, out):
    tall = probs.shape[1]
    mixed = jnp.dot(probs[0], values[0, 0, 0], preferred_element_type=F32) + base[0]
    mixed = mixed.astype(BF16)
    out[0] = jnp.concatenate(
        [mixed[h * steps : (h + 1) * steps] for h in range(tall // steps)], axis=1
    )


def mix(probs, base, cache, steps):
    rows, tall, slots = probs.shape
    width = tall // steps * HD
    return pl.pallas_call(
        functools.partial(mix_kernel, steps),
        grid=(rows,),
        in_specs=[
            pl.BlockSpec((1, tall, slots), lambda r: (r, 0, 0)),
            pl.BlockSpec((1, tall, HD), lambda r: (r, 0, 0)),
            pl.BlockSpec((1, 1, 1, slots, HD), lambda r: (r, 0, 1, 0, 0)),
        ],
        out_specs=pl.BlockSpec((1, steps, width), lambda r: (r, 0, 0)),
        out_shape=jax.ShapeDtypeStruct((rows, steps, width), BF16),
        compiler_params=pltpu.CompilerParams(vmem_limit_bytes=24 * MIB),
        cost_estimate=pl.CostEstimate(
            flops=2 * rows * tall * slots * HD, bytes_accessed=cache.size, transcendentals=0
        ),
        name="mix",
    )(probs, base, in_hbm(cache))


def total(x):
    return jnp.sum(jnp.sum(x, axis=0, keepdims=True), axis=1, keepdims=True)


def ratio_kernel(gathered, ratios, means):
    rows, steps = ratios.shape
    count = rows * steps
    n_fsdp = lax.axis_size("fsdp")
    n_tp = gathered.shape[0] // n_fsdp
    lines = gathered[...].reshape(n_fsdp, n_tp, 128)
    normalizer = jnp.sum(lines, axis=1)[:, :count] / H
    first = lines[:, 0]
    recorded = first[:, count : 2 * count]
    version = first[:, 2 * count : 3 * count]
    ratio = jnp.exp(jnp.clip(normalizer - recorded, -2.0, 2.0))
    lane = lax.broadcasted_iota(jnp.int32, means.shape, 1)
    sums = jnp.zeros(means.shape, F32)
    members = jnp.zeros(means.shape, F32)
    for v in range(VERSIONS):
        hit = version == float(v)
        there = lane == v
        sums = jnp.where(there, total(jnp.where(hit, ratio, 0.0)), sums)
        members = jnp.where(there, total(jnp.where(hit, 1.0, 0.0)), members)
    means[...] = sums / jnp.maximum(members, 1.0)
    group = lax.broadcasted_iota(jnp.int32, ratio.shape, 0)
    mine = jnp.sum(
        jnp.where(group == lax.axis_index("fsdp"), ratio, 0.0), axis=0, keepdims=True
    )
    for r in range(rows):
        ratios[r : r + 1] = mine[:, r * steps : (r + 1) * steps]


def final(gathered, rows, steps):
    return pl.pallas_call(
        ratio_kernel,
        in_specs=[VMEM],
        out_specs=[VMEM, VMEM],
        out_shape=[
            jax.ShapeDtypeStruct((rows, steps), F32),
            jax.ShapeDtypeStruct((1, VERSIONS), F32),
        ],
        name="ratios",
    )(in_vmem(gathered))


def shards(master, moment, second, grad, hidden, cache, lengths, recorded, versions):
    n_tp = lax.axis_size("tp")
    n_fsdp = lax.axis_size("fsdp")
    rows, steps, width = hidden.shape
    tall = rows * steps
    depth = width // n_fsdp
    chips = n_fsdp // 2
    cores = [[i for i in range(n_fsdp) if i % 2 == c] for c in range(2)]

    def move(block, hop):
        return lax.ppermute(block, "fsdp", [(i, i ^ hop) for i in range(n_fsdp)]) if hop else block

    meta, spread = stage(lengths, versions, recorded, hidden, n_fsdp)
    spread = spread.reshape(*(len(hops) for hops in HOPS), tall, depth)
    along_x = [move(spread[k], hop) for k, hop in enumerate(HOPS[0])]

    learned = (master, moment, second, grad)
    fresh = adam(learned, n_tp, (n_tp, master.shape[0], master.shape[1] // n_tp), BF16, "weights")
    fresh, along_x, learned = lax.optimization_barrier((fresh, along_x, learned))
    weights = lax.all_to_all(fresh, "tp", 0, 0, tiled=True).reshape(depth, -1)
    new_master = adam(learned, n_tp, master.shape, F32, "master")

    spread = jnp.stack(along_x)
    along_y = [move(spread[:, k], hop) for k, hop in enumerate(HOPS[1])]
    along_y, new_master = lax.optimization_barrier((along_y, new_master))
    spread = jnp.stack(along_y, axis=1)
    spread = jnp.stack([move(spread[:, :, k], hop) for k, hop in enumerate(HOPS[2])], axis=2)
    spread = spread.reshape(n_fsdp, tall, depth)

    sent = product(spread, weights, n_fsdp, 1)
    arrived = move(sent, 1)
    partial, keys = product(spread, weights, n_fsdp, 0, cache=cache)
    partial = partial + arrived
    parts = lax.all_to_all(
        partial.reshape(chips, tall, -1), "fsdp", 0, 0, tiled=True, axis_index_groups=cores
    )
    probs, base, lines = score(parts, keys, cache, meta, n_fsdp * n_tp)
    lines = lax.all_to_all(lines, ("fsdp", "tp"), 0, 0, tiled=True)
    attention = mix(probs, base, cache, steps)
    ratios, version_means = final(lines, rows, steps)
    return (new_master, attention, ratios, version_means.reshape(VERSIONS))


def solution(mesh):
    in_specs = (
        P(("fsdp", "tp"), None),
        P(("fsdp", "tp"), None),
        P(("fsdp", "tp"), None),
        P(("fsdp", "tp"), None),
        P("fsdp", None, None),
        P("fsdp", "tp", None, None, None),
        P("fsdp"),
        P("fsdp", None),
        P("fsdp"),
    )
    out_specs = (P(("fsdp", "tp"), None), P("fsdp", None, "tp"), P("fsdp", None), P())
    return jax.shard_map(shards, mesh=mesh, in_specs=in_specs, out_specs=out_specs, check_vma=False)
```
